32 devices in a mesh: dp: 2 (over x), expert: 16 (over z, y, core).
Axes of the slice: x: 2, y: 2, z: 4, core: 2. Of those that a mesh axis runs over, the one named last changes fastest.
Arguments:
- tokens: bfloat16 [4096, 512], P(('dp', 'expert')), may hold values from -6 to 6
- modality: int32 [4096], P(('dp', 'expert')), may hold values 0 or 1
- modal_gains: float32 [2, 512], replicated, may hold values from 0.5 to 2
- routes: int32 [4096, 2], P(('dp', 'expert')), may hold values from 0 to 15, all different within a row; in each aligned block of 128 rows (0 to 127, 128 to 255, ...) at most 32 rows name the same one
- gate_share: int32 [4096], P(('dp', 'expert')), may hold values from 1 to 15
- up_weight: bfloat16 [16, 2048, 512], P('expert', 'dp'), may hold values from -0.25 to 0.25
- down_weight: bfloat16 [16, 2048, 512], P('expert', 'dp'), may hold values from -0.125 to 0.125
- cotangent: bfloat16 [4096, 512], P(('dp', 'expert')), may hold values from -6 to 6
Outputs:
- moe_output: bfloat16 [4096, 512], P(('dp', 'expert'))
- token_grad: bfloat16 [4096, 512], P(('dp', 'expert'))
- up_grad: bfloat16 [16, 2048, 512], P('expert', 'dp')
- down_grad: bfloat16 [16, 2048, 512], P('expert', 'dp')
The draws below stay inside these ranges and needn't reach their ends.
Inputs may be any that keep to these rules, and one draw needn't show every extreme that they name: `routes`: each row names two different experts; among the 128 rows of one device no expert is named more than 32 times, and in every draw some device names some expert exactly 32 times.
All inputs are finite; a program needn't handle non-finite values. No bound on the sum of `modality` on one device may be relied on, other than what follows from the above.
Results may differ from the reference program's by a relative error of at most 0.014.
Values may be sent and summed in bfloat16 or wider, within the bound.
A program may use at most 64 MiB of HBM per device.

```python
import math
import jax
import jax.numpy as jnp
import numpy as np
from jax import lax

D = 512
FF = 2048
TOK_DEV = 128
EXPERTS = 16
CAP = 32
SLOTS = 512
GROUP_TOKENS = 2048
TOKENS = 4096
ROUTES_EXPERT = 512
N_DP = 2


def with_ends(result, rng, least, top_value):
    shape = result.shape
    place = [jax.random.randint(jax.random.fold_in(rng, axis), (), 0, shape[axis]) for axis in range(len(shape))]
    result = result.at[tuple(place)].set(least)
    longest = shape.index(max(shape))
    place[longest] = (place[longest] + 1) % shape[longest]
    return result.at[tuple(place)].set(top_value)


def steps_of(own_key, shape, pieces, least, high):
    factor_of, own = 1.0, jax.random.fold_in(own_key, 6)
    for dim, parts in pieces:
        steps = jnp.exp(jax.random.uniform(jax.random.fold_in(own, dim), (parts,), jnp.float32, least / len(pieces), high / len(pieces)))
        factor_of = factor_of * jnp.repeat(steps, shape[dim] // parts).reshape([-1 if axis == dim else 1 for axis in range(len(shape))])
    return factor_of


def routed_block(own_key, own, number, rows, number_of, top, most, lean):
    order = jax.random.permutation(own_key, number_of)
    heavy_load, common = shares(number_of, rows * top, most, lean, True), shares(number_of, rows * top, most, lean, False)
    places = jnp.arange(number_of)

    def named(sizes, offset_by):
        used = int((sizes > 0).sum())
        fixed = max(1, used // 4)
        shifted = fixed + (places - fixed + offset_by * (used - fixed)) % max(1, number_of - fixed)
        return jnp.zeros((number_of,), jnp.int32).at[order[jnp.where(places < fixed, places, shifted)]].set(jnp.asarray(sizes, jnp.int32))

    sizes = jnp.where(number % 4 == 0, named(heavy_load, number // 4), named(common, number - number // 4 - 1))
    mixed = jax.random.permutation(jax.random.fold_in(own, 3), number_of)
    donor, receiver = mixed[0:number_of // 2 * 2:2], mixed[1:number_of // 2 * 2:2]
    margin = jnp.minimum(sizes[donor] - 1, most - sizes[receiver]) // 2
    margin = jnp.where((donor == order[0]) | (receiver == order[0]) | (sizes[receiver] == 0), 0, jnp.maximum(margin, 0))
    shifted = jax.random.randint(jax.random.fold_in(own, 4), (number_of // 2,), 0, 1 << 20) % (margin + 1)
    sizes = sizes.at[donor].add(-shifted).at[receiver].add(shifted)
    items = jnp.searchsorted(jnp.cumsum(sizes), jnp.arange(rows * top), side="right").astype(jnp.int32)
    listing = items.reshape(top, rows).T
    listing = listing[jax.random.permutation(jax.random.fold_in(own, 1), rows)]
    offset_by = jax.random.randint(jax.random.fold_in(own, 2), (rows, 1), 0, top)
    return jnp.take_along_axis(listing, (jnp.arange(top)[None, :] + offset_by) % top, axis=1)


def shares(amount, total, limit, slope, full):
    weights = [(1 << 20) // math.isqrt(standing ** slope) + 1 for standing in range(1, amount + 1)]
    largest = limit if full else min(limit, max(-(-total // amount), total * weights[0] // sum(weights)))
    least = 1 if total - largest >= amount - 1 else 0
    counts, spare = [largest] + [least] * (amount - 1), total - largest - least * (amount - 1)
    while spare > 0:
        candidates = [i for i in range(1, amount) if counts[i] < largest] or [i for i in range(1, amount) if counts[i] < limit]
        mass, left = sum([weights[i] for i in candidates]), spare
        for i in candidates:
            more = min(limit - counts[i], max(1, left * weights[i] // mass), spare)
            counts[i] = counts[i] + more
            spare = spare - more
    return np.array(counts)


def centred(rng, dims, spread, limit, pieces=(), held_as=jnp.bfloat16):
    entries = spread * jax.random.normal(rng, dims, jnp.float32)
    if pieces:
        entries = entries * steps_of(rng, dims, pieces, -0.22, 0.18)
    return jnp.clip(entries, -limit, limit).astype(held_as)


def setup_inputs(seed: int = 0) -> dict:
    arg_keys = jax.random.split(jax.random.key(seed), 9)
    tokens = centred(arg_keys[0], (TOKENS, D), 1.0, 6.0, ((0, 32),))
    modality = with_ends((jax.random.randint(arg_keys[1], (TOKENS,), 0, 2) < 1).astype(jnp.int32), jax.random.fold_in(arg_keys[1], 1), 0, 1)
    modal_gains = jnp.clip(jnp.exp(jax.random.uniform(arg_keys[2], (2, D), jnp.float32, math.log(0.5), math.log(2.0))), 0.5, 2.0)
    routes_keys = jax.random.split(jax.random.fold_in(arg_keys[3], 1), TOKENS // TOK_DEV)
    routes_turns = jax.random.permutation(jax.random.fold_in(arg_keys[3], 3), TOKENS // TOK_DEV)
    routes = jax.vmap(lambda own, number: routed_block(jax.random.fold_in(arg_keys[3], 2), own, number, TOK_DEV, EXPERTS, 2, CAP, 2))(routes_keys, routes_turns).reshape((TOKENS, 2))
    gate_share = with_ends(jax.random.randint(arg_keys[4], (TOKENS,), 1, 16), jax.random.fold_in(arg_keys[4], 1), 1, 15).astype(jnp.int32)
    up_weight = centred(arg_keys[5], (EXPERTS, FF, D), D ** -0.5, 0.25, ((0, 16), (1, 2)))
    down_weight = centred(arg_keys[6], (EXPERTS, FF, D), FF ** -0.5, 0.125, ((0, 16), (1, 2)))
    cotangent = centred(arg_keys[7], (TOKENS, D), 1.0, 6.0, ((0, 32),))
    return {"tokens": tokens, "modality": modality, "modal_gains": modal_gains, "routes": routes, "gate_share": gate_share, "up_weight": up_weight, "down_weight": down_weight, "cotangent": cotangent}


root_half = 0.7071067811865476
density = 0.3989422804014327

def gelu_value(values):
    return values * 0.5 * (1.0 + lax.erf(values * root_half))

def gelu_slope(values):
    return 0.5 * (1.0 + lax.erf(values * root_half)) + values * jnp.exp(-0.5 * values * values) * density

def reference(tokens, modality, modal_gains, routes, gate_share, up_weight, down_weight, cotangent):
    x_float = tokens.astype(jnp.float32)
    inv_rms = lax.rsqrt(lax.optimization_barrier(jnp.mean(x_float * x_float, axis=-1, keepdims=True)) + 1e-06)
    gain_rows = jnp.where(modality[:, None] == 1, modal_gains[1][None, :], modal_gains[0][None, :])
    normed = (x_float * inv_rms * gain_rows).astype(jnp.bfloat16)
    gate_first = gate_share.astype(jnp.float32) / 16.0
    gate_pair = jnp.stack([gate_first, 1.0 - gate_first], axis=1)
    route_grad = (gate_pair[:, :, None] * cotangent.astype(jnp.float32)[:, None, :]).astype(jnp.bfloat16).reshape(-1, D)
    normed_routes = jnp.repeat(normed, 2, axis=0)
    flat_routes = routes.reshape(-1).astype(jnp.int32)
    route_total = flat_routes.shape[0]
    route_ids = jnp.arange(route_total, dtype=jnp.int32)
    group_of = (route_ids // 2 // GROUP_TOKENS).astype(jnp.int32)
    group_key = (group_of * EXPERTS + flat_routes).astype(jnp.int32)
    ordering = jnp.argsort(group_key, stable=True).astype(jnp.int32)
    group_sizes = jax.ops.segment_sum(jnp.ones((route_total,), jnp.int32), group_key, num_segments=N_DP * EXPERTS).astype(jnp.int32)
    group_start = (jnp.cumsum(group_sizes) - group_sizes).astype(jnp.int32)
    rank_sorted = (route_ids - group_start[group_key[ordering]]).astype(jnp.int32)
    route_rank = jnp.zeros((route_total,), jnp.int32).at[ordering].set(rank_sorted)
    slot_ids = jnp.arange(SLOTS, dtype=jnp.int32)
    grad_scale = 1.0 / math.sqrt(ROUTES_EXPERT)

    def per_expert(expert):
        weight_first = up_weight[expert]
        weight_second = down_weight[expert]

        def per_group(totals, group_index):
            group_now = group_index * EXPERTS + expert
            is_valid = slot_ids < group_sizes[group_now]
            picked = ordering[jnp.minimum(group_start[group_now] + slot_ids, route_total - 1)]
            input_rows = jnp.where(is_valid[:, None], normed_routes[picked], jnp.zeros((), jnp.bfloat16))
            grad_rows = jnp.where(is_valid[:, None], route_grad[picked], jnp.zeros((), jnp.bfloat16))
            pre_act = jnp.dot(input_rows, weight_first.T, preferred_element_type=jnp.float32)
            activated = gelu_value(pre_act).astype(jnp.bfloat16)
            expert_rows = jnp.dot(activated, weight_second, preferred_element_type=jnp.float32).astype(jnp.bfloat16)
            hidden_grad = jnp.dot(grad_rows, weight_second.T, preferred_element_type=jnp.float32)
            pre_grad = (hidden_grad * gelu_slope(pre_act)).astype(jnp.bfloat16)
            back_rows = jnp.dot(pre_grad, weight_first, preferred_element_type=jnp.float32).astype(jnp.bfloat16)
            partial_first = (jnp.dot(pre_grad.T, input_rows, preferred_element_type=jnp.float32) * grad_scale).astype(jnp.bfloat16)
            partial_second = (jnp.dot(activated.T, grad_rows, preferred_element_type=jnp.float32) * grad_scale).astype(jnp.bfloat16)
            partial_first, partial_second = lax.optimization_barrier((partial_first, partial_second))
            totals = (totals[0] + partial_first.astype(jnp.float32), totals[1] + partial_second.astype(jnp.float32))
            return (totals, (expert_rows, back_rows))
        zero_grad = jnp.zeros((FF, D), jnp.float32)
        totals, stacked = lax.scan(per_group, (zero_grad, zero_grad), jnp.arange(N_DP, dtype=jnp.int32))
        return (totals[0].astype(jnp.bfloat16), totals[1].astype(jnp.bfloat16), stacked[0], stacked[1])
    up_grad, down_grad, expert_all, back_all = lax.map(per_expert, jnp.arange(EXPERTS, dtype=jnp.int32))
    route_out = expert_all[flat_routes, group_of, route_rank].astype(jnp.float32).reshape(-1, 2, D)
    moe_output = lax.optimization_barrier(jnp.sum(gate_pair[:, :, None] * route_out, axis=1)).astype(jnp.bfloat16)
    normed_grad = lax.optimization_barrier(jnp.sum(back_all[flat_routes, group_of, route_rank].astype(jnp.float32).reshape(-1, 2, D), axis=1))
    scaled = gain_rows * normed_grad
    token_grad = (inv_rms * scaled - x_float * inv_rms ** 3 * lax.optimization_barrier(jnp.mean(x_float * scaled, axis=-1, keepdims=True))).astype(jnp.bfloat16)
    return (moe_output, token_grad, up_grad, down_grad)
```

```python
import math

import jax
import jax.numpy as jnp
from jax import lax
from jax.sharding import PartitionSpec as P

root_half = 0.7071067811865476
density = 0.3989422804014327


def product(left_side, right_side, left_axis, right_axis):
    numbers = (((left_axis,), (right_axis,)), ((), ()))
    return lax.dot_general(left_side, right_side, numbers, preferred_element_type=jnp.float32)


def on_device(tokens, modality, modal_gains, routes, gate_share, up_weight, down_weight, cotangent):
    tok_count, width = tokens.shape
    expert_count = lax.axis_size("expert")
    replica_count = lax.axis_size("dp")
    capacity = 4 * tok_count // expert_count
    slot_count = expert_count * capacity
    grad_scale = 1.0 / math.sqrt(2 * tok_count * replica_count)
    up = up_weight[0]
    down = down_weight[0]
    x_float = tokens.astype(jnp.float32)
    inv_rms = lax.rsqrt(jnp.mean(x_float * x_float, axis=-1, keepdims=True) + 1e-06)
    gain_rows = jnp.where(modality[:, None] == 1, modal_gains[1][None, :], modal_gains[0][None, :])
    normed = (x_float * inv_rms * gain_rows).astype(jnp.bfloat16)
    gate_first = gate_share.astype(jnp.float32)[:, None] / 16.0
    column = lax.broadcasted_iota(jnp.int32, (tok_count, slot_count), 1)
    is_first = routes[:, 0:1] == column // capacity
    is_second = routes[:, 1:2] == column // capacity
    named = (is_first | is_second).astype(jnp.bfloat16)
    earlier = (
        lax.broadcasted_iota(jnp.int32, (tok_count, tok_count), 1)
        < lax.broadcasted_iota(jnp.int32, (tok_count, tok_count), 0)
    ).astype(jnp.bfloat16)
    position = product(earlier, named, 1, 0)
    here = (is_first | is_second) & (position == (column % capacity).astype(jnp.float32))
    slot_pick = here.astype(jnp.bfloat16)
    slot_gate = jnp.where(here, jnp.where(is_first, gate_first, 1.0 - gate_first), 0.0).astype(
        jnp.bfloat16
    )
    send = jnp.concatenate(
        [
            product(slot_pick, normed, 0, 0).astype(jnp.bfloat16),
            product(slot_gate, cotangent, 0, 0).astype(jnp.bfloat16),
        ],
        axis=1,
    ).reshape(expert_count, capacity, 2 * width)
    arrived = lax.all_to_all(send, "expert", split_axis=0, concat_axis=0, tiled=True)
    both = lax.all_gather(arrived.reshape(slot_count, 2 * width), "dp", axis=0, tiled=True)
    rows, grads = both[:, :width], both[:, width:]
    pre_act = product(rows, up, 1, 1)
    cdf = 0.5 * (1.0 + lax.erf(pre_act * root_half))
    activated = (pre_act * cdf).astype(jnp.bfloat16)
    hidden_grad = product(grads, down, 1, 1)
    slope = cdf + pre_act * jnp.exp(-0.5 * pre_act * pre_act) * density
    pre_grad = (hidden_grad * slope).astype(jnp.bfloat16)
    parts = jnp.concatenate(
        [
            product(activated, down, 1, 0).astype(jnp.bfloat16),
            product(pre_grad, up, 1, 0).astype(jnp.bfloat16),
        ],
        axis=1,
    )
    summed = lax.psum_scatter(parts, "dp", scatter_dimension=0, tiled=True)
    back = lax.all_to_all(
        summed.reshape(expert_count, capacity, 2 * width),
        "expert",
        split_axis=0,
        concat_axis=0,
        tiled=True,
    ).reshape(slot_count, 2 * width)
    up_grad = (product(pre_grad, rows, 0, 0) * grad_scale).astype(jnp.bfloat16)[None]
    down_grad = (product(activated, grads, 0, 0) * grad_scale).astype(jnp.bfloat16)[None]
    moe_output = product(slot_gate, back[:, :width], 1, 0).astype(jnp.bfloat16)
    scaled = gain_rows * product(slot_pick, back[:, width:], 1, 0)
    token_grad = (
        inv_rms * scaled - x_float * inv_rms**3 * jnp.mean(x_float * scaled, axis=-1, keepdims=True)
    ).astype(jnp.bfloat16)
    return (moe_output, token_grad, up_grad, down_grad)


def solution(mesh):
    token_rows = P(("dp", "expert"), None)
    token_list = P(("dp", "expert"))
    weights = P("expert", "dp", None)
    return jax.shard_map(
        on_device,
        mesh=mesh,
        in_specs=(
            token_rows,
            token_list,
            P(),
            token_rows,
            token_list,
            weights,
            weights,
            token_rows,
        ),
        out_specs=(token_rows, token_rows, weights, weights),
        check_vma=False,
    )
```

```python
import functools
import math

import jax
import jax.numpy as jnp
from jax import lax
from jax.experimental import pallas as pl
from jax.experimental.pallas import tpu as pltpu
from jax.sharding import PartitionSpec as P

root_half = 0.7071067811865476
density = 0.3989422804014327
MESH = pl.DeviceIdType.MESH


def product(left_side, right_side, left_axis, right_axis):
    numbers = (((left_axis,), (right_axis,)), ((), ()))
    return lax.dot_general(left_side, right_side, numbers, preferred_element_type=jnp.float32)


def layer_kernel(
    experts,
    replicas,
    chunks,
    tokens,
    modality,
    gains,
    routes,
    gate_share,
    up,
    down,
    cotangent,
    moe_output,
    token_grad,
    up_grad,
    down_grad,
    send,
    recv,
    parts,
    part_recv,
    own,
    outgoing,
    back,
    act,
    pre_grad,
    slot_pick,
    slot_gate,
    in_send,
    in_recv,
    fwd_send,
    fwd_recv,
    part_send_sem,
    part_recv_sem,
    back_send,
    back_recv,
):
    me = lax.axis_index("expert")
    dp = lax.axis_index("dp")
    tok_count, width = tokens.shape
    capacity = send.shape[1]
    slot_count = experts * capacity
    group = experts // chunks
    chunk_rows = group * capacity
    hidden = up.shape[0]
    hidden_tile = min(256, hidden)
    grad_scale = 1.0 / math.sqrt(2 * tok_count * replicas)
    bits = experts.bit_length() - 1

    def peer(offset):
        total = 0
        for bit in range(bits):
            unit = 1 << bit
            total = total + ((me // unit + offset // unit) % 2) * unit
        return total

    def in_copy(s):
        return pltpu.make_async_remote_copy(
            src_ref=send.at[s],
            dst_ref=recv.at[0, s],
            send_sem=in_send.at[s],
            recv_sem=in_recv.at[s],
            device_id={"expert": peer(s)},
            device_id_type=MESH,
        )

    def back_copy(s):
        return pltpu.make_async_remote_copy(
            src_ref=outgoing.at[s],
            dst_ref=back.at[s],
            send_sem=back_send.at[s],
            recv_sem=back_recv.at[s],
            device_id={"expert": peer(s)},
            device_id_type=MESH,
        )

    def fwd_copy(q, c):
        span = pl.ds(c * group, group)
        return pltpu.make_async_remote_copy(
            src_ref=recv.at[0, span],
            dst_ref=recv.at[q, span],
            send_sem=fwd_send.at[q - 1, c],
            recv_sem=fwd_recv.at[q - 1, c],
            device_id={"dp": (dp + q) % replicas},
            device_id_type=MESH,
        )

    def part_copy(q, c):
        span = pl.ds(c * group, group)
        return pltpu.make_async_remote_copy(
            src_ref=parts.at[q - 1, span],
            dst_ref=part_recv.at[q - 1, span],
            send_sem=part_send_sem.at[q - 1, c],
            recv_sem=part_recv_sem.at[q - 1, c],
            device_id={"dp": (dp + replicas - q) % replicas},
            device_id_type=MESH,
        )

    barrier = pltpu.get_barrier_semaphore()

    @pl.loop(1, experts)
    def _(s):
        pl.semaphore_signal(barrier, inc=1, device_id={"expert": peer(s)}, device_id_type=MESH)

    for q in range(1, replicas):
        pl.semaphore_signal(
            barrier, inc=1, device_id={"dp": (dp + q) % replicas}, device_id_type=MESH
        )

    def norm_parts():
        x_float = tokens[...].astype(jnp.float32)
        inv_rms = lax.rsqrt(jnp.mean(x_float * x_float, axis=-1, keepdims=True) + 1e-06)
        is_text = jnp.broadcast_to(modality[...], (tok_count, width)) == 1
        gain_rows = jnp.where(is_text, gains[1:2, :], gains[0:1, :])
        return x_float, inv_rms, gain_rows

    x_float, inv_rms, gain_rows = norm_parts()
    normed = (x_float * inv_rms * gain_rows).astype(jnp.bfloat16)
    column = lax.broadcasted_iota(jnp.int32, (tok_count, slot_count), 1)
    column_expert = (column // capacity) ^ me
    is_first = jnp.broadcast_to(routes[:, 0:1], column.shape) == column_expert
    is_second = jnp.broadcast_to(routes[:, 1:2], column.shape) == column_expert
    named = jnp.where(is_first | is_second, 1.0, 0.0)
    earlier = jnp.where(
        lax.broadcasted_iota(jnp.int32, (tok_count, tok_count), 1)
        < lax.broadcasted_iota(jnp.int32, (tok_count, tok_count), 0),
        1.0,
        0.0,
    )
    position = product(earlier.astype(jnp.bfloat16), named.astype(jnp.bfloat16), 1, 0)
    place = (column % capacity).astype(jnp.float32)
    pick = jnp.where(position == place, named, 0.0)
    first = jnp.broadcast_to(gate_share[...].astype(jnp.float32) / 16.0, column.shape)
    gate = pick * jnp.where(is_first, first, 1.0 - first)
    slot_pick[...] = pick.astype(jnp.bfloat16)
    slot_gate[...] = gate.astype(jnp.bfloat16)
    send[:, :, :width] = (
        product(slot_pick[...], normed, 0, 0)
        .reshape(experts, capacity, width)
        .astype(jnp.bfloat16)
    )
    send[:, :, width:] = (
        product(slot_gate[...], cotangent[...], 0, 0)
        .reshape(experts, capacity, width)
        .astype(jnp.bfloat16)
    )

    pl.semaphore_wait(barrier, experts + replicas - 2)

    @pl.loop(1, experts)
    def _(s):
        in_copy(s).start()

    recv[0, 0] = send[0]

    def take_in(c):
        for j in range(group):
            s = c * group + j
            if j == 0:

                @pl.when(c > 0)
                def _():
                    in_copy(s).wait_recv()
            else:
                in_copy(s).wait_recv()
        for q in range(1, replicas):
            fwd_copy(q, c).start()

    def work(c):
        span = pl.ds(c * group, group)
        place_rows = pl.ds(pl.multiple_of(c * chunk_rows, chunk_rows), chunk_rows)
        for q in range(1, replicas):
            fwd_copy(q, c).wait_recv()

        def gathered(low):
            return jnp.concatenate(
                [
                    recv[q, span, :, low : low + width].reshape(chunk_rows, width)
                    for q in range(replicas)
                ],
                axis=0,
            )

        rows, grads = gathered(0), gathered(width)
        for low in range(0, hidden, hidden_tile):
            high = low + hidden_tile
            pre_act = product(rows, up[low:high, :], 1, 1)
            hidden_grad = product(grads, down[low:high, :], 1, 1)
            cdf = 0.5 * (1.0 + lax.erf(pre_act * root_half))
            activated = (pre_act * cdf).astype(jnp.bfloat16)
            slope = cdf + pre_act * jnp.exp(-0.5 * pre_act * pre_act) * density
            grad = (hidden_grad * slope).astype(jnp.bfloat16)
            for q in range(replicas):
                part = slice(q * chunk_rows, (q + 1) * chunk_rows)
                act[q, place_rows, low:high] = activated[part]
                pre_grad[q, place_rows, low:high] = grad[part]

        for store, weight, low in ((act, down, 0), (pre_grad, up, width)):
            values = jnp.concatenate([store[q, place_rows, :] for q in range(replicas)], axis=0)
            result = product(values, weight[...], 1, 0)
            own[place_rows, low : low + width] = result[:chunk_rows]
            for q in range(1, replicas):
                part = result[q * chunk_rows : (q + 1) * chunk_rows]
                parts[q - 1, span, :, low : low + width] = part.reshape(
                    group, capacity, width
                ).astype(jnp.bfloat16)
        for q in range(1, replicas):
            part_copy(q, c).start()

    def give_back(c):
        span = pl.ds(c * group, group)
        place_rows = pl.ds(pl.multiple_of(c * chunk_rows, chunk_rows), chunk_rows)
        for q in range(1, replicas):
            part_copy(q, c).wait_recv()
        total = own[place_rows, :].reshape(group, capacity, 2 * width)
        for q in range(1, replicas):
            total = total + part_recv[q - 1, span].astype(jnp.float32)
        outgoing[span] = total.astype(jnp.bfloat16)
        for j in range(group):
            s = c * group + j
            if j == 0:

                @pl.when(c > 0)
                def _():
                    back_copy(s).start()
            else:
                back_copy(s).start()

    @pl.loop(0, chunks + 2)
    def _(t):
        @pl.when(t < chunks)
        def _():
            take_in(t)

        @pl.when((t >= 1) & (t < chunks + 1))
        def _():
            work(t - 1)

        @pl.when(t >= 2)
        def _():
            give_back(t - 2)

    back[0] = outgoing[0]

    for low in range(0, hidden, hidden_tile):
        high = low + hidden_tile
        for store, target, left in ((pre_grad, up_grad, 0), (act, down_grad, width)):
            total = 0.0
            for q in range(replicas):
                rows = recv[q, :, :, left : left + width].reshape(slot_count, width)
                total = total + product(store[q, :, low:high], rows, 0, 0)
            target[low:high, :] = (total * grad_scale).astype(jnp.bfloat16)

    @pl.loop(1, experts)
    def _(s):
        back_copy(s).wait_recv()

    returned = back[:, :, :width].reshape(slot_count, width)
    moe_output[...] = product(slot_gate[...], returned, 1, 0).astype(jnp.bfloat16)
    x_float, inv_rms, gain_rows = norm_parts()
    returned = back[:, :, width:].reshape(slot_count, width)
    scaled = gain_rows * product(slot_pick[...], returned, 1, 0)
    inner = jnp.mean(x_float * scaled, axis=-1, keepdims=True)
    token_grad[...] = (
        inv_rms * scaled - x_float * (inv_rms * inv_rms * inv_rms) * inner
    ).astype(jnp.bfloat16)

    @pl.loop(1, experts)
    def _(s):
        in_copy(s).wait_send()
        back_copy(s).wait_send()

    @pl.loop(0, chunks)
    def _(c):
        for q in range(1, replicas):
            fwd_copy(q, c).wait_send()
            part_copy(q, c).wait_send()


def on_device(tokens, modality, modal_gains, routes, gate_share, up_weight, down_weight, cotangent):
    tok_count, width = tokens.shape
    experts = lax.axis_size("expert")
    replicas = lax.axis_size("dp")
    capacity = 4 * tok_count // experts
    slots = experts * capacity
    hidden = up_weight.shape[1]
    chunks = 4
    half = jnp.bfloat16
    blocks = (experts, capacity, 2 * width)
    dma = pltpu.SemaphoreType.DMA
    in_vmem = pl.BlockSpec(memory_space=pltpu.VMEM)
    moe_output, token_grad, up_grad, down_grad = pl.pallas_call(
        functools.partial(layer_kernel, experts, replicas, chunks),
        out_shape=(
            jax.ShapeDtypeStruct((tok_count, width), half),
            jax.ShapeDtypeStruct((tok_count, width), half),
            jax.ShapeDtypeStruct((hidden, width), half),
            jax.ShapeDtypeStruct((hidden, width), half),
        ),
        in_specs=[in_vmem] * 8,
        out_specs=(in_vmem,) * 4,
        scratch_shapes=[
            pltpu.VMEM(blocks, half),
            pltpu.VMEM((replicas,) + blocks, half),
            pltpu.VMEM((replicas - 1,) + blocks, half),
            pltpu.VMEM((replicas - 1,) + blocks, half),
            pltpu.VMEM((slots, 2 * width), jnp.float32),
            pltpu.VMEM(blocks, half),
            pltpu.VMEM(blocks, half),
            pltpu.VMEM((replicas, slots, hidden), half),
            pltpu.VMEM((replicas, slots, hidden), half),
            pltpu.VMEM((tok_count, slots), half),
            pltpu.VMEM((tok_count, slots), half),
            dma((experts,)),
            dma((experts,)),
            dma((replicas - 1, chunks)),
            dma((replicas - 1, chunks)),
            dma((replicas - 1, chunks)),
            dma((replicas - 1, chunks)),
            dma((experts,)),
            dma((experts,)),
        ],
        compiler_params=pltpu.CompilerParams(
            collective_id=0, has_side_effects=True, vmem_limit_bytes=56 * 1024 * 1024
        ),
    )(
        tokens,
        modality[:, None],
        modal_gains,
        routes,
        gate_share[:, None],
        up_weight[0],
        down_weight[0],
        cotangent,
    )
    return (moe_output, token_grad, up_grad[None], down_grad[None])


def solution(mesh):
    token_rows = P(("dp", "expert"), None)
    token_list = P(("dp", "expert"))
    weights = P("expert", "dp", None)
    return jax.shard_map(
        on_device,
        mesh=mesh,
        in_specs=(
            token_rows,
            token_list,
            P(),
            token_rows,
            token_list,
            weights,
            weights,
            token_rows,
        ),
        out_specs=(token_rows, token_rows, weights, weights),
        check_vma=False,
    )
```

```python
import functools
import math

import jax
import jax.numpy as jnp
from jax import lax
from jax.experimental import pallas as pl
from jax.experimental.pallas import tpu as pltpu
from jax.sharding import PartitionSpec as P

root_half = 0.7071067811865476
density = 0.3989422804014327
MESH = pl.DeviceIdType.MESH


def product(left_side, right_side, left_axis, right_axis):
    numbers = (((left_axis,), (right_axis,)), ((), ()))
    return lax.dot_general(left_side, right_side, numbers, preferred_element_type=jnp.float32)


def layer_kernel(
    experts,
    replicas,
    chunks,
    tokens,
    modality,
    gains,
    routes,
    gate_share,
    up,
    down,
    cotangent,
    moe_output,
    token_grad,
    up_grad,
    down_grad,
    send,
    recv,
    parts,
    part_recv,
    own,
    outgoing,
    back,
    act,
    pre_grad,
    slot_pick,
    slot_gate,
    in_send,
    in_recv,
    fwd_send,
    fwd_recv,
    part_send_sem,
    part_recv_sem,
    back_send,
    back_recv,
):
    me = lax.axis_index("expert")
    dp = lax.axis_index("dp")
    tok_count, width = tokens.shape
    capacity = send.shape[1]
    slot_count = experts * capacity
    group = experts // chunks
    chunk_rows = group * capacity
    hidden = up.shape[0]
    hidden_tile = min(256, hidden)
    grad_scale = 1.0 / math.sqrt(2 * tok_count * replicas)
    bits = experts.bit_length() - 1

    def peer(offset):
        total = 0
        for bit in range(bits):
            unit = 1 << bit
            total = total + ((me // unit + offset // unit) % 2) * unit
        return total

    def turn(t):
        step = t // (chunks // 4)
        return (2 * step + 3 * (step // 2)) % 4 * (chunks // 4) + t % (chunks // 4)

    def unless_own(c, j, act_on):
        if j == 0:

            @pl.when(c > 0)
            def _():
                act_on(c * group)
        else:
            act_on(c * group + j)

    def in_copy(s):
        return pltpu.make_async_remote_copy(
            src_ref=send.at[s],
            dst_ref=recv.at[0, s],
            send_sem=in_send.at[s],
            recv_sem=in_recv.at[s],
            device_id={"expert": peer(s)},
            device_id_type=MESH,
        )

    def back_copy(s):
        return pltpu.make_async_remote_copy(
            src_ref=outgoing.at[s],
            dst_ref=back.at[s],
            send_sem=back_send.at[s],
            recv_sem=back_recv.at[s],
            device_id={"expert": peer(s)},
            device_id_type=MESH,
        )

    def fwd_copy(q, c):
        span = pl.ds(c * group, group)
        return pltpu.make_async_remote_copy(
            src_ref=recv.at[0, span],
            dst_ref=recv.at[q, span],
            send_sem=fwd_send.at[q - 1, c],
            recv_sem=fwd_recv.at[q - 1, c],
            device_id={"dp": (dp + q) % replicas},
            device_id_type=MESH,
        )

    def part_copy(q, c):
        span = pl.ds(c * group, group)
        return pltpu.make_async_remote_copy(
            src_ref=parts.at[q - 1, span],
            dst_ref=part_recv.at[q - 1, span],
            send_sem=part_send_sem.at[q - 1, c],
            recv_sem=part_recv_sem.at[q - 1, c],
            device_id={"dp": (dp + replicas - q) % replicas},
            device_id_type=MESH,
        )

    barrier = pltpu.get_barrier_semaphore()

    @pl.loop(1, experts)
    def _(s):
        pl.semaphore_signal(barrier, inc=1, device_id={"expert": peer(s)}, device_id_type=MESH)

    for q in range(1, replicas):
        pl.semaphore_signal(
            barrier, inc=1, device_id={"dp": (dp + q) % replicas}, device_id_type=MESH
        )

    marks = jnp.concatenate(
        [modality[...], routes[...], gate_share[...], jnp.zeros((4, tok_count), jnp.int32)], axis=0
    )
    marks = marks.astype(jnp.float32).T.astype(jnp.int32)

    def norm_parts():
        x_float = tokens[...].astype(jnp.float32)
        inv_rms = lax.rsqrt(jnp.mean(x_float * x_float, axis=-1, keepdims=True) + 1e-06)
        is_text = jnp.broadcast_to(marks[:, 0:1], (tok_count, width)) == 1
        gain_rows = jnp.where(is_text, gains[1:2, :], gains[0:1, :])
        return x_float, inv_rms, gain_rows

    x_float, inv_rms, gain_rows = norm_parts()
    normed = (x_float * inv_rms * gain_rows).astype(jnp.bfloat16)
    column = lax.broadcasted_iota(jnp.int32, (tok_count, slot_count), 1)
    column_expert = (column // capacity) ^ me
    is_first = jnp.broadcast_to(marks[:, 1:2], column.shape) == column_expert
    is_second = jnp.broadcast_to(marks[:, 2:3], column.shape) == column_expert
    named = jnp.where(is_first | is_second, 1.0, 0.0)
    earlier = jnp.where(
        lax.broadcasted_iota(jnp.int32, (tok_count, tok_count), 1)
        < lax.broadcasted_iota(jnp.int32, (tok_count, tok_count), 0),
        1.0,
        0.0,
    )
    position = product(earlier.astype(jnp.bfloat16), named.astype(jnp.bfloat16), 1, 0)
    place = (column % capacity).astype(jnp.float32)
    pick = jnp.where(position == place, named, 0.0)
    first = jnp.broadcast_to(marks[:, 3:4].astype(jnp.float32) / 16.0, column.shape)
    gate = pick * jnp.where(is_first, first, 1.0 - first)
    slot_pick[...] = pick.astype(jnp.bfloat16)
    slot_gate[...] = gate.astype(jnp.bfloat16)
    send[:, :, :width] = (
        product(slot_pick[...], normed, 0, 0)
        .reshape(experts, capacity, width)
        .astype(jnp.bfloat16)
    )
    send[:, :, width:] = (
        product(slot_gate[...], cotangent[...], 0, 0)
        .reshape(experts, capacity, width)
        .astype(jnp.bfloat16)
    )

    pl.semaphore_wait(barrier, experts + replicas - 2)

    recv[0, 0] = send[0]

    @pl.loop(0, chunks)
    def _(t):
        c = turn(t)
        for j in range(group):
            unless_own(c, j, lambda s: in_copy(s).start())

    def take_in(c):
        for j in range(group):
            unless_own(c, j, lambda s: in_copy(s).wait_recv())
        for q in range(1, replicas):
            fwd_copy(q, c).start()

    def work(c):
        span = pl.ds(c * group, group)
        place_rows = pl.ds(pl.multiple_of(c * chunk_rows, chunk_rows), chunk_rows)
        for q in range(1, replicas):
            fwd_copy(q, c).wait_recv()

        def gathered(low):
            return jnp.concatenate(
                [
                    recv[q, span, :, low : low + width].reshape(chunk_rows, width)
                    for q in range(replicas)
                ],
                axis=0,
            )

        rows, grads = gathered(0), gathered(width)
        for low in range(0, hidden, hidden_tile):
            high = low + hidden_tile
            pre_act = product(rows, up[low:high, :], 1, 1)
            hidden_grad = product(grads, down[low:high, :], 1, 1)
            cdf = 0.5 * (1.0 + lax.erf(pre_act * root_half))
            activated = (pre_act * cdf).astype(jnp.bfloat16)
            slope = cdf + pre_act * jnp.exp(-0.5 * pre_act * pre_act) * density
            grad = (hidden_grad * slope).astype(jnp.bfloat16)
            for q in range(replicas):
                part = slice(q * chunk_rows, (q + 1) * chunk_rows)
                act[q, place_rows, low:high] = activated[part]
                pre_grad[q, place_rows, low:high] = grad[part]

        for store, weight, low in ((act, down, 0), (pre_grad, up, width)):
            values = jnp.concatenate([store[q, place_rows, :] for q in range(replicas)], axis=0)
            result = product(values, weight[...], 1, 0)
            own[place_rows, low : low + width] = result[:chunk_rows]
            for q in range(1, replicas):
                part = result[q * chunk_rows : (q + 1) * chunk_rows]
                parts[q - 1, span, :, low : low + width] = part.reshape(
                    group, capacity, width
                ).astype(jnp.bfloat16)
        for q in range(1, replicas):
            part_copy(q, c).start()

    def give_back(c):
        span = pl.ds(c * group, group)
        place_rows = pl.ds(pl.multiple_of(c * chunk_rows, chunk_rows), chunk_rows)
        for q in range(1, replicas):
            part_copy(q, c).wait_recv()
        total = own[place_rows, :].reshape(group, capacity, 2 * width)
        for q in range(1, replicas):
            total = total + part_recv[q - 1, span].astype(jnp.float32)
        outgoing[span] = total.astype(jnp.bfloat16)
        for j in range(group):
            unless_own(c, j, lambda s: back_copy(s).start())

    @pl.loop(0, chunks + 2)
    def _(t):
        @pl.when(t < chunks)
        def _():
            take_in(turn(t))

        @pl.when((t >= 1) & (t < chunks + 1))
        def _():
            work(turn(t - 1))

        @pl.when(t >= 2)
        def _():
            give_back(turn(t - 2))

    back[0] = outgoing[0]

    for low in range(0, hidden, hidden_tile):
        high = low + hidden_tile
        for store, target, left in ((pre_grad, up_grad, 0), (act, down_grad, width)):
            total = 0.0
            for q in range(replicas):
                rows = recv[q, :, :, left : left + width].reshape(slot_count, width)
                total = total + product(store[q, :, low:high], rows, 0, 0)
            target[low:high, :] = (total * grad_scale).astype(jnp.bfloat16)

    @pl.loop(1, experts)
    def _(s):
        back_copy(s).wait_recv()

    returned = back[:, :, :width].reshape(slot_count, width)
    moe_output[...] = product(slot_gate[...], returned, 1, 0).astype(jnp.bfloat16)
    x_float, inv_rms, gain_rows = norm_parts()
    returned = back[:, :, width:].reshape(slot_count, width)
    scaled = gain_rows * product(slot_pick[...], returned, 1, 0)
    inner = jnp.mean(x_float * scaled, axis=-1, keepdims=True)
    token_grad[...] = (
        inv_rms * scaled - x_float * (inv_rms * inv_rms * inv_rms) * inner
    ).astype(jnp.bfloat16)

    @pl.loop(1, experts)
    def _(s):
        in_copy(s).wait_send()
        back_copy(s).wait_send()

    @pl.loop(0, chunks)
    def _(c):
        for q in range(1, replicas):
            fwd_copy(q, c).wait_send()
            part_copy(q, c).wait_send()


def on_device(tokens, modality, modal_gains, routes, gate_share, up_weight, down_weight, cotangent):
    tok_count, width = tokens.shape
    experts = lax.axis_size("expert")
    replicas = lax.axis_size("dp")
    capacity = 4 * tok_count // experts
    slots = experts * capacity
    hidden = up_weight.shape[1]
    chunks = 8
    half = jnp.bfloat16
    blocks = (experts, capacity, 2 * width)
    dma = pltpu.SemaphoreType.DMA
    in_vmem = pl.BlockSpec(memory_space=pltpu.VMEM)
    moe_output, token_grad, up_grad, down_grad = pl.pallas_call(
        functools.partial(layer_kernel, experts, replicas, chunks),
        out_shape=(
            jax.ShapeDtypeStruct((tok_count, width), half),
            jax.ShapeDtypeStruct((tok_count, width), half),
            jax.ShapeDtypeStruct((hidden, width), half),
            jax.ShapeDtypeStruct((hidden, width), half),
        ),
        in_specs=[in_vmem] * 8,
        out_specs=(in_vmem,) * 4,
        scratch_shapes=[
            pltpu.VMEM(blocks, half),
            pltpu.VMEM((replicas,) + blocks, half),
            pltpu.VMEM((replicas - 1,) + blocks, half),
            pltpu.VMEM((replicas - 1,) + blocks, half),
            pltpu.VMEM((slots, 2 * width), jnp.float32),
            pltpu.VMEM(blocks, half),
            pltpu.VMEM(blocks, half),
            pltpu.VMEM((replicas, slots, hidden), half),
            pltpu.VMEM((replicas, slots, hidden), half),
            pltpu.VMEM((tok_count, slots), half),
            pltpu.VMEM((tok_count, slots), half),
            dma((experts,)),
            dma((experts,)),
            dma((replicas - 1, chunks)),
            dma((replicas - 1, chunks)),
            dma((replicas - 1, chunks)),
            dma((replicas - 1, chunks)),
            dma((experts,)),
            dma((experts,)),
        ],
        compiler_params=pltpu.CompilerParams(
            collective_id=0, has_side_effects=True, vmem_limit_bytes=56 * 1024 * 1024
        ),
    )(
        tokens,
        modality[None],
        modal_gains,
        routes.T,
        gate_share[None],
        up_weight[0],
        down_weight[0],
        cotangent,
    )
    return (moe_output, token_grad, up_grad[None], down_grad[None])


def solution(mesh):
    token_rows = P(("dp", "expert"), None)
    token_list = P(("dp", "expert"))
    weights = P("expert", "dp", None)
    return jax.shard_map(
        on_device,
        mesh=mesh,
        in_specs=(
            token_rows,
            token_list,
            P(),
            token_rows,
            token_list,
            weights,
            weights,
            token_rows,
        ),
        out_specs=(token_rows, token_rows, weights, weights),
        check_vma=False,
    )
```

```python
import functools
import math

import jax
import jax.numpy as jnp
from jax import lax
from jax.experimental import pallas as pl
from jax.experimental.pallas import tpu as pltpu
from jax.sharding import PartitionSpec as P

root_half = 0.7071067811865476
density = 0.3989422804014327
MESH = pl.DeviceIdType.MESH


def product(left_side, right_side, left_axis, right_axis):
    numbers = (((left_axis,), (right_axis,)), ((), ()))
    return lax.dot_general(left_side, right_side, numbers, preferred_element_type=jnp.float32)


def layer_kernel(
    experts,
    replicas,
    chunks,
    tokens,
    modality,
    gains,
    routes,
    gate_share,
    up,
    down,
    cotangent,
    moe_output,
    token_grad,
    up_grad,
    down_grad,
    send,
    recv,
    parts,
    part_recv,
    own,
    outgoing,
    back,
    act,
    pre_grad,
    slot_pick,
    slot_gate,
    in_send,
    in_recv,
    fwd_send,
    fwd_recv,
    part_send_sem,
    part_recv_sem,
    back_send,
    back_recv,
    marks_out,
    marks_in,
    dense_out,
    dense_in,
    near_send,
    near_back,
    sums_out,
    sums_in,
    other_pick,
    other_gate,
    dense_sems,
    marks_sems,
    sums_sems,
    near_sems,
    return_sems,
):
    me = lax.axis_index("expert")
    dp = lax.axis_index("dp")
    tok_count, width = tokens.shape
    capacity = send.shape[1]
    slot_count = experts * capacity
    group = experts // chunks
    chunk_rows = group * capacity
    hidden = up.shape[0]
    hidden_tile = min(256, hidden)
    grad_scale = 1.0 / math.sqrt(2 * tok_count * replicas)
    bits = experts.bit_length() - 1

    def peer(offset):
        total = 0
        for bit in range(bits):
            unit = 1 << bit
            total = total + ((me // unit + offset // unit) % 2) * unit
        return total

    def turn(t):
        step = (t // (chunks // 4) + 3) % 4
        quarter = step // 2 * 2 + (step % 2 + step // 2) % 2
        return quarter * (chunks // 4) + t % (chunks // 4)

    def unless_own(c, j, act_on):
        if j == 0:

            @pl.when(c > 0)
            def _():
                act_on(c * group)
        else:
            act_on(c * group + j)

    def in_copy(s):
        return pltpu.make_async_remote_copy(
            src_ref=send.at[s],
            dst_ref=recv.at[0, s],
            send_sem=in_send.at[s],
            recv_sem=in_recv.at[s],
            device_id={"expert": peer(s)},
            device_id_type=MESH,
        )

    def back_copy(s):
        return pltpu.make_async_remote_copy(
            src_ref=outgoing.at[s],
            dst_ref=back.at[s],
            send_sem=back_send.at[s],
            recv_sem=back_recv.at[s],
            device_id={"expert": peer(s)},
            device_id_type=MESH,
        )

    def over_dp(source, target, sems, q, step):
        return pltpu.make_async_remote_copy(
            src_ref=source,
            dst_ref=target.at[q - 1],
            send_sem=sems.at[0, q - 1],
            recv_sem=sems.at[1, q - 1],
            device_id={"dp": (dp + step) % replicas},
            device_id_type=MESH,
        )

    def dense_copy(q):
        return over_dp(dense_out, dense_in, dense_sems, q, q)

    def marks_copy(q):
        return over_dp(marks_out, marks_in, marks_sems, q, q)

    def sums_copy(q):
        return over_dp(sums_out.at[q - 1], sums_in, sums_sems, q, replicas - q)

    def near_copy(q, s):
        return pltpu.make_async_remote_copy(
            src_ref=near_send.at[q - 1, s],
            dst_ref=recv.at[q, s],
            send_sem=near_sems.at[0, q - 1, s],
            recv_sem=near_sems.at[1, q - 1, s],
            device_id={"expert": peer(s)},
            device_id_type=MESH,
        )

    def return_copy(q, s):
        return pltpu.make_async_remote_copy(
            src_ref=parts.at[q - 1, s],
            dst_ref=near_back.at[q - 1, s],
            send_sem=return_sems.at[0, q - 1, s],
            recv_sem=return_sems.at[1, q - 1, s],
            device_id={"expert": peer(s)},
            device_id_type=MESH,
        )

    def fwd_copy(q, c):
        span = pl.ds(c * group, group)
        return pltpu.make_async_remote_copy(
            src_ref=recv.at[0, span],
            dst_ref=recv.at[q, span],
            send_sem=fwd_send.at[q - 1, c],
            recv_sem=fwd_recv.at[q - 1, c],
            device_id={"dp": (dp + q) % replicas},
            device_id_type=MESH,
        )

    def part_copy(q, c):
        span = pl.ds(c * group, group)
        return pltpu.make_async_remote_copy(
            src_ref=parts.at[q - 1, span],
            dst_ref=part_recv.at[q - 1, span],
            send_sem=part_send_sem.at[q - 1, c],
            recv_sem=part_recv_sem.at[q - 1, c],
            device_id={"dp": (dp + replicas - q) % replicas},
            device_id_type=MESH,
        )

    barrier = pltpu.get_barrier_semaphore()

    @pl.loop(1, experts)
    def _(s):
        pl.semaphore_signal(barrier, inc=1, device_id={"expert": peer(s)}, device_id_type=MESH)

    for q in range(1, replicas):
        pl.semaphore_signal(
            barrier, inc=1, device_id={"dp": (dp + q) % replicas}, device_id_type=MESH
        )

    marks_out[...] = jnp.concatenate(
        [modality[...], routes[...], gate_share[...], jnp.zeros((4, tok_count), jnp.int32)], axis=0
    )
    marks = marks_out[...].astype(jnp.float32).T.astype(jnp.int32)

    def norm_parts():
        x_float = tokens[...].astype(jnp.float32)
        inv_rms = lax.rsqrt(jnp.mean(x_float * x_float, axis=-1, keepdims=True) + 1e-06)
        is_text = jnp.broadcast_to(marks[:, 0:1], (tok_count, width)) == 1
        gain_rows = jnp.where(is_text, gains[1:2, :], gains[0:1, :])
        return x_float, inv_rms, gain_rows

    x_float, inv_rms, gain_rows = norm_parts()
    normed = (x_float * inv_rms * gain_rows).astype(jnp.bfloat16)
    dense_out[:, :width] = normed
    dense_out[:, width:] = cotangent[...]
    pl.semaphore_wait(barrier, experts + replicas - 2)
    for q in range(1, replicas):
        marks_copy(q).start()
        dense_copy(q).start()

    def slots_of(numbers, columns):
        column = lax.broadcasted_iota(jnp.int32, (tok_count, columns), 1)
        column_expert = (column // capacity) ^ me
        is_first = jnp.broadcast_to(numbers[:, 1:2], column.shape) == column_expert
        is_second = jnp.broadcast_to(numbers[:, 2:3], column.shape) == column_expert
        named = jnp.where(is_first | is_second, 1.0, 0.0)
        earlier = jnp.where(
            lax.broadcasted_iota(jnp.int32, (tok_count, tok_count), 1)
            < lax.broadcasted_iota(jnp.int32, (tok_count, tok_count), 0),
            1.0,
            0.0,
        )
        position = product(earlier.astype(jnp.bfloat16), named.astype(jnp.bfloat16), 1, 0)
        place = (column % capacity).astype(jnp.float32)
        pick = jnp.where(position == place, named, 0.0)
        first = jnp.broadcast_to(numbers[:, 3:4].astype(jnp.float32) / 16.0, column.shape)
        gate = pick * jnp.where(is_first, first, 1.0 - first)
        return pick.astype(jnp.bfloat16), gate.astype(jnp.bfloat16)

    def slot_blocks(chosen, values):
        blocks = product(chosen, values, 0, 0).astype(jnp.bfloat16)
        return blocks.reshape(-1, capacity, width)

    slot_pick[...], slot_gate[...] = slots_of(marks, slot_count)
    send[:, :, :width] = slot_blocks(slot_pick[...], normed)
    send[:, :, width:] = slot_blocks(slot_gate[...], cotangent[...])

    recv[0, 0] = send[0]

    @pl.loop(0, chunks)
    def _(t):
        c = turn(t)
        for j in range(group):
            unless_own(c, j, lambda s: in_copy(s).start())

    near = experts // 2
    near_chunks = chunks // 2
    for q in range(1, replicas):
        marks_copy(q).wait_recv()
        numbers = marks_in[q - 1].astype(jnp.float32).T.astype(jnp.int32)
        pick, gate = slots_of(numbers, near * capacity)
        other_pick[q - 1] = pick
        other_gate[q - 1] = gate
        dense_copy(q).wait_recv()
        near_send[q - 1, :, :, :width] = slot_blocks(pick, dense_in[q - 1, :, :width])
        near_send[q - 1, :, :, width:] = slot_blocks(gate, dense_in[q - 1, :, width:])
        recv[q, 0] = near_send[q - 1, 0]

        @pl.loop(1, near)
        def _(s):
            near_copy(q, s).start()

    def take_in(c):
        for j in range(group):
            unless_own(c, j, lambda s: in_copy(s).wait_recv())

        @pl.when(c >= near_chunks)
        def _():
            for q in range(1, replicas):
                fwd_copy(q, c).start()

    def work(c):
        span = pl.ds(c * group, group)
        place_rows = pl.ds(pl.multiple_of(c * chunk_rows, chunk_rows), chunk_rows)

        @pl.when(c >= near_chunks)
        def _():
            for q in range(1, replicas):
                fwd_copy(q, c).wait_recv()

        @pl.when(c < near_chunks)
        def _():
            for q in range(1, replicas):
                for j in range(group):
                    unless_own(c, j, lambda s: near_copy(q, s).wait_recv())

        def gathered(low):
            return jnp.concatenate(
                [
                    recv[q, span, :, low : low + width].reshape(chunk_rows, width)
                    for q in range(replicas)
                ],
                axis=0,
            )

        rows, grads = gathered(0), gathered(width)
        for low in range(0, hidden, hidden_tile):
            high = low + hidden_tile
            pre_act = product(rows, up[low:high, :], 1, 1)
            hidden_grad = product(grads, down[low:high, :], 1, 1)
            cdf = 0.5 * (1.0 + lax.erf(pre_act * root_half))
            activated = (pre_act * cdf).astype(jnp.bfloat16)
            slope = cdf + pre_act * jnp.exp(-0.5 * pre_act * pre_act) * density
            grad = (hidden_grad * slope).astype(jnp.bfloat16)
            for q in range(replicas):
                part = slice(q * chunk_rows, (q + 1) * chunk_rows)
                act[q, place_rows, low:high] = activated[part]
                pre_grad[q, place_rows, low:high] = grad[part]

        for store, weight, low in ((act, down, 0), (pre_grad, up, width)):
            values = jnp.concatenate([store[q, place_rows, :] for q in range(replicas)], axis=0)
            result = product(values, weight[...], 1, 0)
            own[place_rows, low : low + width] = result[:chunk_rows]
            for q in range(1, replicas):
                part = result[q * chunk_rows : (q + 1) * chunk_rows]
                parts[q - 1, span, :, low : low + width] = part.reshape(
                    group, capacity, width
                ).astype(jnp.bfloat16)

        @pl.when(c >= near_chunks)
        def _():
            for q in range(1, replicas):
                part_copy(q, c).start()

        @pl.when(c < near_chunks)
        def _():
            for q in range(1, replicas):
                for j in range(group):
                    unless_own(c, j, lambda s: return_copy(q, s).start())

    def give_back(c):
        span = pl.ds(c * group, group)
        place_rows = pl.ds(pl.multiple_of(c * chunk_rows, chunk_rows), chunk_rows)
        total = own[place_rows, :].reshape(group, capacity, 2 * width)

        @pl.when(c < near_chunks)
        def _():
            outgoing[span] = total.astype(jnp.bfloat16)

        @pl.when(c >= near_chunks)
        def _():
            whole = total
            for q in range(1, replicas):
                part_copy(q, c).wait_recv()
                whole = whole + part_recv[q - 1, span].astype(jnp.float32)
            outgoing[span] = whole.astype(jnp.bfloat16)

        for j in range(group):
            unless_own(c, j, lambda s: back_copy(s).start())

    @pl.loop(0, chunks + 2)
    def _(t):
        @pl.when(t < chunks)
        def _():
            take_in(turn(t))

        @pl.when((t >= 1) & (t < chunks + 1))
        def _():
            work(turn(t - 1))

        @pl.when(t >= 2)
        def _():
            give_back(turn(t - 2))

    back[0] = outgoing[0]

    for q in range(1, replicas):
        near_back[q - 1, 0] = parts[q - 1, 0]

        @pl.loop(1, near)
        def _(s):
            return_copy(q, s).wait_recv()

        for chosen, low in ((other_gate, 0), (other_pick, width)):
            values = near_back[q - 1, :, :, low : low + width].reshape(near * capacity, width)
            sums_out[q - 1, :, low : low + width] = product(chosen[q - 1], values, 1, 0).astype(
                jnp.bfloat16
            )
        sums_copy(q).start()

    for low in range(0, hidden, hidden_tile):
        high = low + hidden_tile
        for store, target, left in ((pre_grad, up_grad, 0), (act, down_grad, width)):
            total = 0.0
            for q in range(replicas):
                rows = recv[q, :, :, left : left + width].reshape(slot_count, width)
                total = total + product(store[q, :, low:high], rows, 0, 0)
            target[low:high, :] = (total * grad_scale).astype(jnp.bfloat16)

    @pl.loop(1, experts)
    def _(s):
        back_copy(s).wait_recv()

    for q in range(1, replicas):
        sums_copy(q).wait_recv()

    def combined(chosen, low):
        returned = back[:, :, low : low + width].reshape(slot_count, width)
        total = product(chosen[...], returned, 1, 0)
        for q in range(1, replicas):
            total = total + sums_in[q - 1, :, low : low + width].astype(jnp.float32)
        return total

    moe_output[...] = combined(slot_gate, 0).astype(jnp.bfloat16)
    x_float, inv_rms, gain_rows = norm_parts()
    scaled = gain_rows * combined(slot_pick, width)
    inner = jnp.mean(x_float * scaled, axis=-1, keepdims=True)
    token_grad[...] = (
        inv_rms * scaled - x_float * (inv_rms * inv_rms * inv_rms) * inner
    ).astype(jnp.bfloat16)

    @pl.loop(1, experts)
    def _(s):
        in_copy(s).wait_send()
        back_copy(s).wait_send()

    for q in range(1, replicas):
        marks_copy(q).wait_send()
        dense_copy(q).wait_send()
        sums_copy(q).wait_send()

        @pl.loop(1, near)
        def _(s):
            near_copy(q, s).wait_send()
            return_copy(q, s).wait_send()

        @pl.loop(near_chunks, chunks)
        def _(c):
            fwd_copy(q, c).wait_send()
            part_copy(q, c).wait_send()


def on_device(tokens, modality, modal_gains, routes, gate_share, up_weight, down_weight, cotangent):
    tok_count, width = tokens.shape
    experts = lax.axis_size("expert")
    replicas = lax.axis_size("dp")
    capacity = 4 * tok_count // experts
    slots = experts * capacity
    hidden = up_weight.shape[1]
    chunks = 8
    half = jnp.bfloat16
    blocks = (experts, capacity, 2 * width)
    dma = pltpu.SemaphoreType.DMA
    in_vmem = pl.BlockSpec(memory_space=pltpu.VMEM)
    moe_output, token_grad, up_grad, down_grad = pl.pallas_call(
        functools.partial(layer_kernel, experts, replicas, chunks),
        out_shape=(
            jax.ShapeDtypeStruct((tok_count, width), half),
            jax.ShapeDtypeStruct((tok_count, width), half),
            jax.ShapeDtypeStruct((hidden, width), half),
            jax.ShapeDtypeStruct((hidden, width), half),
        ),
        in_specs=[in_vmem] * 8,
        out_specs=(in_vmem,) * 4,
        scratch_shapes=[
            pltpu.VMEM(blocks, half),
            pltpu.VMEM((replicas,) + blocks, half),
            pltpu.VMEM((replicas - 1,) + blocks, half),
            pltpu.VMEM((replicas - 1,) + blocks, half),
            pltpu.VMEM((slots, 2 * width), jnp.float32),
            pltpu.VMEM(blocks, half),
            pltpu.VMEM(blocks, half),
            pltpu.VMEM((replicas, slots, hidden), half),
            pltpu.VMEM((replicas, slots, hidden), half),
            pltpu.VMEM((tok_count, slots), half),
            pltpu.VMEM((tok_count, slots), half),
            dma((experts,)),
            dma((experts,)),
            dma((replicas - 1, chunks)),
            dma((replicas - 1, chunks)),
            dma((replicas - 1, chunks)),
            dma((replicas - 1, chunks)),
            dma((experts,)),
            dma((experts,)),
            pltpu.VMEM((8, tok_count), jnp.int32),
            pltpu.VMEM((replicas - 1, 8, tok_count), jnp.int32),
            pltpu.VMEM((tok_count, 2 * width), half),
            pltpu.VMEM((replicas - 1, tok_count, 2 * width), half),
            pltpu.VMEM((replicas - 1, experts // 2, capacity, 2 * width), half),
            pltpu.VMEM((replicas - 1, experts // 2, capacity, 2 * width), half),
            pltpu.VMEM((replicas - 1, tok_count, 2 * width), half),
            pltpu.VMEM((replicas - 1, tok_count, 2 * width), half),
            pltpu.VMEM((replicas - 1, tok_count, slots // 2), half),
            pltpu.VMEM((replicas - 1, tok_count, slots // 2), half),
            dma((2, replicas - 1)),
            dma((2, replicas - 1)),
            dma((2, replicas - 1)),
            dma((2, replicas - 1, experts // 2)),
            dma((2, replicas - 1, experts // 2)),
        ],
        compiler_params=pltpu.CompilerParams(
            collective_id=0, has_side_effects=True, vmem_limit_bytes=56 * 1024 * 1024
        ),
    )(
        tokens,
        modality[None],
        modal_gains,
        routes.T,
        gate_share[None],
        up_weight[0],
        down_weight[0],
        cotangent,
    )
    return (moe_output, token_grad, up_grad[None], down_grad[None])


def solution(mesh):
    token_rows = P(("dp", "expert"), None)
    token_list = P(("dp", "expert"))
    weights = P("expert", "dp", None)
    return jax.shard_map(
        on_device,
        mesh=mesh,
        in_specs=(
            token_rows,
            token_list,
            P(),
            token_rows,
            token_list,
            weights,
            weights,
            token_rows,
        ),
        out_specs=(token_rows, token_rows, weights, weights),
        check_vma=False,
    )
```

```python
import functools
import math

import jax
import jax.numpy as jnp
from jax import lax
from jax.experimental import pallas as pl
from jax.experimental.pallas import tpu as pltpu
from jax.sharding import PartitionSpec as P

root_half = 0.7071067811865476
density = 0.3989422804014327
MESH = pl.DeviceIdType.MESH


def product(left_side, right_side, left_axis, right_axis):
    numbers = (((left_axis,), (right_axis,)), ((), ()))
    return lax.dot_general(left_side, right_side, numbers, preferred_element_type=jnp.float32)


def layer_kernel(
    experts,
    replicas,
    chunks,
    tokens,
    modality,
    gains,
    routes,
    gate_share,
    up_home,
    down_home,
    cotangent,
    moe_output,
    token_grad,
    up_out,
    down_out,
    send,
    recv,
    parts,
    part_recv,
    own,
    outgoing,
    back,
    act,
    pre_grad,
    slot_pick,
    slot_gate,
    in_send,
    in_recv,
    fwd_send,
    fwd_recv,
    part_send_sem,
    part_recv_sem,
    back_send,
    back_recv,
    marks_out,
    marks_in,
    dense_out,
    dense_in,
    near_send,
    near_back,
    sums_out,
    sums_in,
    other_pick,
    other_gate,
    dense_sems,
    marks_sems,
    sums_sems,
    near_sems,
    return_sems,
    up,
    down,
    up_grad,
    down_grad,
    local_sems,
):
    me = lax.axis_index("expert")
    dp = lax.axis_index("dp")
    tok_count, width = tokens.shape
    capacity = send.shape[1]
    slot_count = experts * capacity
    group = experts // chunks
    chunk_rows = group * capacity
    hidden = up.shape[0]
    hidden_tile = min(256, hidden)
    grad_scale = 1.0 / math.sqrt(2 * tok_count * replicas)
    bits = experts.bit_length() - 1

    def peer(offset):
        total = 0
        for bit in range(bits):
            unit = 1 << bit
            total = total + ((me // unit + offset // unit) % 2) * unit
        return total

    def turn(t):
        step = (t // (chunks // 4) + 3) % 4
        quarter = step // 2 * 2 + (step % 2 + step // 2) % 2
        return quarter * (chunks // 4) + t % (chunks // 4)

    def unless_own(c, j, act_on):
        if j == 0:

            @pl.when(c > 0)
            def _():
                act_on(c * group)
        else:
            act_on(c * group + j)

    def in_copy(s):
        return pltpu.make_async_remote_copy(
            src_ref=send.at[s],
            dst_ref=recv.at[0, s],
            send_sem=in_send.at[s],
            recv_sem=in_recv.at[s],
            device_id={"expert": peer(s)},
            device_id_type=MESH,
        )

    def back_copy(s):
        return pltpu.make_async_remote_copy(
            src_ref=outgoing.at[s],
            dst_ref=back.at[s],
            send_sem=back_send.at[s],
            recv_sem=back_recv.at[s],
            device_id={"expert": peer(s)},
            device_id_type=MESH,
        )

    def over_dp(source, target, sems, q, step):
        return pltpu.make_async_remote_copy(
            src_ref=source,
            dst_ref=target.at[q - 1],
            send_sem=sems.at[0, q - 1],
            recv_sem=sems.at[1, q - 1],
            device_id={"dp": (dp + step) % replicas},
            device_id_type=MESH,
        )

    def dense_copy(q):
        return over_dp(dense_out, dense_in, dense_sems, q, q)

    def marks_copy(q):
        return over_dp(marks_out, marks_in, marks_sems, q, q)

    def sums_copy(q):
        return over_dp(sums_out.at[q - 1], sums_in, sums_sems, q, replicas - q)

    def near_copy(q, s):
        return pltpu.make_async_remote_copy(
            src_ref=near_send.at[q - 1, s],
            dst_ref=recv.at[q, s],
            send_sem=near_sems.at[0, q - 1, s],
            recv_sem=near_sems.at[1, q - 1, s],
            device_id={"expert": peer(s)},
            device_id_type=MESH,
        )

    def return_copy(q, s):
        return pltpu.make_async_remote_copy(
            src_ref=parts.at[q - 1, s],
            dst_ref=near_back.at[q - 1, s],
            send_sem=return_sems.at[0, q - 1, s],
            recv_sem=return_sems.at[1, q - 1, s],
            device_id={"expert": peer(s)},
            device_id_type=MESH,
        )

    def fwd_copy(q, c):
        span = pl.ds(c * group, group)
        return pltpu.make_async_remote_copy(
            src_ref=recv.at[0, span],
            dst_ref=recv.at[q, span],
            send_sem=fwd_send.at[q - 1, c],
            recv_sem=fwd_recv.at[q - 1, c],
            device_id={"dp": (dp + q) % replicas},
            device_id_type=MESH,
        )

    def part_copy(q, c):
        span = pl.ds(c * group, group)
        return pltpu.make_async_remote_copy(
            src_ref=parts.at[q - 1, span],
            dst_ref=part_recv.at[q - 1, span],
            send_sem=part_send_sem.at[q - 1, c],
            recv_sem=part_recv_sem.at[q - 1, c],
            device_id={"dp": (dp + replicas - q) % replicas},
            device_id_type=MESH,
        )

    up_load = pltpu.make_async_copy(up_home, up, local_sems.at[0])
    down_load = pltpu.make_async_copy(down_home, down, local_sems.at[1])
    up_store = pltpu.make_async_copy(up_grad, up_out, local_sems.at[2])
    down_store = pltpu.make_async_copy(down_grad, down_out, local_sems.at[3])
    up_load.start()
    down_load.start()

    barrier = pltpu.get_barrier_semaphore()

    @pl.loop(1, experts)
    def _(s):
        pl.semaphore_signal(barrier, inc=1, device_id={"expert": peer(s)}, device_id_type=MESH)

    for q in range(1, replicas):
        pl.semaphore_signal(
            barrier, inc=1, device_id={"dp": (dp + q) % replicas}, device_id_type=MESH
        )

    marks_out[...] = jnp.concatenate(
        [modality[...], routes[...], gate_share[...], jnp.zeros((4, tok_count), jnp.int32)], axis=0
    )
    marks = marks_out[...].astype(jnp.float32).T.astype(jnp.int32)

    def norm_parts():
        x_float = tokens[...].astype(jnp.float32)
        inv_rms = lax.rsqrt(jnp.mean(x_float * x_float, axis=-1, keepdims=True) + 1e-06)
        is_text = jnp.broadcast_to(marks[:, 0:1], (tok_count, width)) == 1
        gain_rows = jnp.where(is_text, gains[1:2, :], gains[0:1, :])
        return x_float, inv_rms, gain_rows

    x_float, inv_rms, gain_rows = norm_parts()
    normed = (x_float * inv_rms * gain_rows).astype(jnp.bfloat16)
    dense_out[:, :width] = normed
    dense_out[:, width:] = cotangent[...]
    pl.semaphore_wait(barrier, experts + replicas - 2)
    for q in range(1, replicas):
        marks_copy(q).start()
        dense_copy(q).start()

    def slots_of(numbers, columns):
        column = lax.broadcasted_iota(jnp.int32, (tok_count, columns), 1)
        column_expert = (column // capacity) ^ me
        is_first = jnp.broadcast_to(numbers[:, 1:2], column.shape) == column_expert
        is_second = jnp.broadcast_to(numbers[:, 2:3], column.shape) == column_expert
        named = jnp.where(is_first | is_second, 1.0, 0.0)
        earlier = jnp.where(
            lax.broadcasted_iota(jnp.int32, (tok_count, tok_count), 1)
            < lax.broadcasted_iota(jnp.int32, (tok_count, tok_count), 0),
            1.0,
            0.0,
        )
        position = product(earlier.astype(jnp.bfloat16), named.astype(jnp.bfloat16), 1, 0)
        place = (column % capacity).astype(jnp.float32)
        pick = jnp.where(position == place, named, 0.0)
        first = jnp.broadcast_to(numbers[:, 3:4].astype(jnp.float32) / 16.0, column.shape)
        gate = pick * jnp.where(is_first, first, 1.0 - first)
        return pick.astype(jnp.bfloat16), gate.astype(jnp.bfloat16)

    def slot_blocks(chosen, values):
        blocks = product(chosen, values, 0, 0).astype(jnp.bfloat16)
        return blocks.reshape(-1, capacity, width)

    slot_pick[...], slot_gate[...] = slots_of(marks, slot_count)
    send[:, :, :width] = slot_blocks(slot_pick[...], normed)
    send[:, :, width:] = slot_blocks(slot_gate[...], cotangent[...])

    recv[0, 0] = send[0]

    @pl.loop(0, chunks)
    def _(t):
        c = turn(t)
        for j in range(group):
            unless_own(c, j, lambda s: in_copy(s).start())

    near = experts // 2
    near_chunks = chunks // 2
    for q in range(1, replicas):
        marks_copy(q).wait_recv()
        numbers = marks_in[q - 1].astype(jnp.float32).T.astype(jnp.int32)
        pick, gate = slots_of(numbers, near * capacity)
        other_pick[q - 1] = pick
        other_gate[q - 1] = gate
        dense_copy(q).wait_recv()
        near_send[q - 1, :, :, :width] = slot_blocks(pick, dense_in[q - 1, :, :width])
        near_send[q - 1, :, :, width:] = slot_blocks(gate, dense_in[q - 1, :, width:])
        recv[q, 0] = near_send[q - 1, 0]

        @pl.loop(1, near)
        def _(s):
            near_copy(q, s).start()

    def take_in(c):
        for j in range(group):
            unless_own(c, j, lambda s: in_copy(s).wait_recv())

        @pl.when(c >= near_chunks)
        def _():
            for q in range(1, replicas):
                fwd_copy(q, c).start()

    def work(c):
        span = pl.ds(c * group, group)
        place_rows = pl.ds(pl.multiple_of(c * chunk_rows, chunk_rows), chunk_rows)

        @pl.when(c >= near_chunks)
        def _():
            for q in range(1, replicas):
                fwd_copy(q, c).wait_recv()

        @pl.when(c < near_chunks)
        def _():
            for q in range(1, replicas):
                for j in range(group):
                    unless_own(c, j, lambda s: near_copy(q, s).wait_recv())

        def gathered(low):
            return jnp.concatenate(
                [
                    recv[q, span, :, low : low + width].reshape(chunk_rows, width)
                    for q in range(replicas)
                ],
                axis=0,
            )

        rows, grads = gathered(0), gathered(width)
        for low in range(0, hidden, hidden_tile):
            high = low + hidden_tile
            pre_act = product(rows, up[low:high, :], 1, 1)
            hidden_grad = product(grads, down[low:high, :], 1, 1)
            cdf = 0.5 * (1.0 + lax.erf(pre_act * root_half))
            activated = (pre_act * cdf).astype(jnp.bfloat16)
            slope = cdf + pre_act * jnp.exp(-0.5 * pre_act * pre_act) * density
            grad = (hidden_grad * slope).astype(jnp.bfloat16)
            for q in range(replicas):
                part = slice(q * chunk_rows, (q + 1) * chunk_rows)
                act[q, place_rows, low:high] = activated[part]
                pre_grad[q, place_rows, low:high] = grad[part]

        for store, weight, low in ((act, down, 0), (pre_grad, up, width)):
            values = jnp.concatenate([store[q, place_rows, :] for q in range(replicas)], axis=0)
            result = product(values, weight[...], 1, 0)
            own[place_rows, low : low + width] = result[:chunk_rows]
            for q in range(1, replicas):
                part = result[q * chunk_rows : (q + 1) * chunk_rows]
                parts[q - 1, span, :, low : low + width] = part.reshape(
                    group, capacity, width
                ).astype(jnp.bfloat16)

        @pl.when(c >= near_chunks)
        def _():
            for q in range(1, replicas):
                part_copy(q, c).start()

        @pl.when(c < near_chunks)
        def _():
            for q in range(1, replicas):
                for j in range(group):
                    unless_own(c, j, lambda s: return_copy(q, s).start())

    def give_back(c):
        span = pl.ds(c * group, group)
        place_rows = pl.ds(pl.multiple_of(c * chunk_rows, chunk_rows), chunk_rows)
        total = own[place_rows, :].reshape(group, capacity, 2 * width)

        @pl.when(c < near_chunks)
        def _():
            outgoing[span] = total.astype(jnp.bfloat16)

        @pl.when(c >= near_chunks)
        def _():
            whole = total
            for q in range(1, replicas):
                part_copy(q, c).wait_recv()
                whole = whole + part_recv[q - 1, span].astype(jnp.float32)
            outgoing[span] = whole.astype(jnp.bfloat16)

        for j in range(group):
            unless_own(c, j, lambda s: back_copy(s).start())

    up_load.wait()
    down_load.wait()

    @pl.loop(0, chunks + 2)
    def _(t):
        @pl.when(t < chunks)
        def _():
            take_in(turn(t))

        @pl.when((t >= 1) & (t < chunks + 1))
        def _():
            work(turn(t - 1))

        @pl.when(t >= 2)
        def _():
            give_back(turn(t - 2))

    back[0] = outgoing[0]

    for q in range(1, replicas):
        near_back[q - 1, 0] = parts[q - 1, 0]

        @pl.loop(1, near)
        def _(s):
            return_copy(q, s).wait_recv()

        for chosen, low in ((other_gate, 0), (other_pick, width)):
            values = near_back[q - 1, :, :, low : low + width].reshape(near * capacity, width)
            sums_out[q - 1, :, low : low + width] = product(chosen[q - 1], values, 1, 0).astype(
                jnp.bfloat16
            )
        sums_copy(q).start()

    for low in range(0, hidden, hidden_tile):
        high = low + hidden_tile
        for store, target, left in ((pre_grad, up_grad, 0), (act, down_grad, width)):
            total = 0.0
            for q in range(replicas):
                rows = recv[q, :, :, left : left + width].reshape(slot_count, width)
                total = total + product(store[q, :, low:high], rows, 0, 0)
            target[low:high, :] = (total * grad_scale).astype(jnp.bfloat16)

    up_store.start()
    down_store.start()

    @pl.loop(1, experts)
    def _(s):
        back_copy(s).wait_recv()

    for q in range(1, replicas):
        sums_copy(q).wait_recv()

    def combined(chosen, low):
        returned = back[:, :, low : low + width].reshape(slot_count, width)
        total = product(chosen[...], returned, 1, 0)
        for q in range(1, replicas):
            total = total + sums_in[q - 1, :, low : low + width].astype(jnp.float32)
        return total

    moe_output[...] = combined(slot_gate, 0).astype(jnp.bfloat16)
    x_float, inv_rms, gain_rows = norm_parts()
    scaled = gain_rows * combined(slot_pick, width)
    inner = jnp.mean(x_float * scaled, axis=-1, keepdims=True)
    token_grad[...] = (
        inv_rms * scaled - x_float * (inv_rms * inv_rms * inv_rms) * inner
    ).astype(jnp.bfloat16)

    up_store.wait()
    down_store.wait()

    @pl.loop(1, experts)
    def _(s):
        in_copy(s).wait_send()
        back_copy(s).wait_send()

    for q in range(1, replicas):
        marks_copy(q).wait_send()
        dense_copy(q).wait_send()
        sums_copy(q).wait_send()

        @pl.loop(1, near)
        def _(s):
            near_copy(q, s).wait_send()
            return_copy(q, s).wait_send()

        @pl.loop(near_chunks, chunks)
        def _(c):
            fwd_copy(q, c).wait_send()
            part_copy(q, c).wait_send()


def on_device(tokens, modality, modal_gains, routes, gate_share, up_weight, down_weight, cotangent):
    tok_count, width = tokens.shape
    experts = lax.axis_size("expert")
    replicas = lax.axis_size("dp")
    capacity = 4 * tok_count // experts
    slots = experts * capacity
    hidden = up_weight.shape[1]
    chunks = 8
    half = jnp.bfloat16
    blocks = (experts, capacity, 2 * width)
    dma = pltpu.SemaphoreType.DMA
    in_vmem = pl.BlockSpec(memory_space=pltpu.VMEM)
    anywhere = pl.BlockSpec(memory_space=pl.ANY)
    moe_output, token_grad, up_grad, down_grad = pl.pallas_call(
        functools.partial(layer_kernel, experts, replicas, chunks),
        out_shape=(
            jax.ShapeDtypeStruct((tok_count, width), half),
            jax.ShapeDtypeStruct((tok_count, width), half),
            jax.ShapeDtypeStruct((hidden, width), half),
            jax.ShapeDtypeStruct((hidden, width), half),
        ),
        in_specs=[in_vmem] * 5 + [anywhere] * 2 + [in_vmem],
        out_specs=(in_vmem, in_vmem, anywhere, anywhere),
        scratch_shapes=[
            pltpu.VMEM(blocks, half),
            pltpu.VMEM((replicas,) + blocks, half),
            pltpu.VMEM((replicas - 1,) + blocks, half),
            pltpu.VMEM((replicas - 1,) + blocks, half),
            pltpu.VMEM((slots, 2 * width), jnp.float32),
            pltpu.VMEM(blocks, half),
            pltpu.VMEM(blocks, half),
            pltpu.VMEM((replicas, slots, hidden), half),
            pltpu.VMEM((replicas, slots, hidden), half),
            pltpu.VMEM((tok_count, slots), half),
            pltpu.VMEM((tok_count, slots), half),
            dma((experts,)),
            dma((experts,)),
            dma((replicas - 1, chunks)),
            dma((replicas - 1, chunks)),
            dma((replicas - 1, chunks)),
            dma((replicas - 1, chunks)),
            dma((experts,)),
            dma((experts,)),
            pltpu.VMEM((8, tok_count), jnp.int32),
            pltpu.VMEM((replicas - 1, 8, tok_count), jnp.int32),
            pltpu.VMEM((tok_count, 2 * width), half),
            pltpu.VMEM((replicas - 1, tok_count, 2 * width), half),
            pltpu.VMEM((replicas - 1, experts // 2, capacity, 2 * width), half),
            pltpu.VMEM((replicas - 1, experts // 2, capacity, 2 * width), half),
            pltpu.VMEM((replicas - 1, tok_count, 2 * width), half),
            pltpu.VMEM((replicas - 1, tok_count, 2 * width), half),
            pltpu.VMEM((replicas - 1, tok_count, slots // 2), half),
            pltpu.VMEM((replicas - 1, tok_count, slots // 2), half),
            dma((2, replicas - 1)),
            dma((2, replicas - 1)),
            dma((2, replicas - 1)),
            dma((2, replicas - 1, experts // 2)),
            dma((2, replicas - 1, experts // 2)),
            pltpu.VMEM((hidden, width), half),
            pltpu.VMEM((hidden, width), half),
            pltpu.VMEM((hidden, width), half),
            pltpu.VMEM((hidden, width), half),
            dma((4,)),
        ],
        compiler_params=pltpu.CompilerParams(
            collective_id=0, has_side_effects=True, vmem_limit_bytes=min(56, 12 + 10 * replicas) * 1024 * 1024
        ),
    )(
        tokens,
        modality[None],
        modal_gains,
        routes.T,
        gate_share[None],
        up_weight[0],
        down_weight[0],
        cotangent,
    )
    return (moe_output, token_grad, up_grad[None], down_grad[None])


def solution(mesh):
    token_rows = P(("dp", "expert"), None)
    token_list = P(("dp", "expert"))
    weights = P("expert", "dp", None)
    return jax.shard_map(
        on_device,
        mesh=mesh,
        in_specs=(
            token_rows,
            token_list,
            P(),
            token_rows,
            token_list,
            weights,
            weights,
            token_rows,
        ),
        out_specs=(token_rows, token_rows, weights, weights),
        check_vma=False,
    )
```
